32 devices in a mesh: rows: 8 (over z, x), tm: 4 (over y, core).
Axes of the slice: x: 2, y: 2, z: 4, core: 2. Of those that a mesh axis runs over, the one named last changes fastest.
Arguments:
- raw_signal: float32 [256, 64, 128], P('tm', 'rows'), may hold values from -6 to 6
- fir_taps: float32 [61], replicated, may hold values from -0.75 to 0.75
- white_coef: float32 [25, 64, 128], P(None, 'rows'), may hold values from -1.25 to 1.25
- templates: bfloat16 [64, 61, 25], replicated, may hold values from -0.15625 to 0.15625
Outputs:
- whitened: bfloat16 [256, 64, 128], P('tm', 'rows')
- best_score: float32 [256, 64, 128], P('tm', 'rows')
The draws below stay inside these ranges and needn't reach their ends.
All inputs are finite; a program needn't handle non-finite values.
Results may differ from the reference program's by a relative error of at most 0.0049.
Values may be sent and summed in bfloat16 or wider, within the bound.
A program may use at most 64 MiB of HBM per device.

```python
import jax
import jax.numpy as jnp
from jax import lax

COLS = 128
TEMPLATES = 64
TAPS = 61
TLEN = 61
TIME = 256
GRID_ROWS = 64


def levels(stream_key, extent, shards, least, largest):
    def one(axis_at, blocks):
        draws = jax.random.uniform(jax.random.fold_in(jax.random.fold_in(stream_key, 6), axis_at), (blocks,), jnp.float32, least / len(shards), largest / len(shards))
        return jnp.repeat(jnp.exp(draws), extent[axis_at] // blocks).reshape((-1,) + (1,) * (len(extent) - axis_at - 1))

    factor_of = one(*shards[0])
    for cut in shards[1:]:
        factor_of = factor_of * one(*cut)
    return factor_of


def normal_values(own_key, extent, scale, limit, shards=(), held_as=jnp.bfloat16):
    factor_of = levels(own_key, extent, shards, -0.22, 0.18) if shards else 1.0
    result = jax.random.normal(own_key, extent, jnp.float32) * scale * factor_of
    return jnp.minimum(jnp.maximum(result, -limit), limit).astype(held_as)


def setup_inputs(seed: int = 0) -> dict:
    streams_of = jax.random.split(jax.random.key(seed), 5)
    raw_signal = normal_values(streams_of[0], (TIME, GRID_ROWS, COLS), 1.0, 6.0, ((0, 4), (1, 8)), jnp.float32)
    fir_taps = normal_values(streams_of[1], (TAPS,), TAPS ** -0.5, 0.75, (), jnp.float32)
    white_coef = normal_values(streams_of[2], (25, GRID_ROWS, COLS), 25 ** -0.5, 1.25, ((1, 8),), jnp.float32)
    templates = normal_values(streams_of[3], (TEMPLATES, TLEN, 25), (25 * TLEN) ** -0.5, 0.15625)
    return dict(raw_signal=raw_signal, fir_taps=fir_taps, white_coef=white_coef, templates=templates)


def template_bands(templates, block_len):
    by_spot = jnp.transpose(templates, (0, 2, 1))
    tmpl_len = templates.shape[1]
    shifted = [jnp.pad(by_spot, ((0, 0), (0, 0), (b, block_len - 1 - b))) for b in range(block_len)]
    stacked = jnp.stack(shifted, axis=1)
    return stacked.reshape(templates.shape[0] * block_len, 25 * (tmpl_len + block_len - 1))


def reference(raw_signal, fir_taps, white_coef, templates):
    num_steps, grid_rows, col_count = raw_signal.shape
    taps_back = fir_taps.shape[0] - 1
    padded = jnp.pad(raw_signal, ((taps_back, 0), (0, 0), (0, 0)))
    filt_sum = jnp.zeros(raw_signal.shape, jnp.float32)
    for k in range(taps_back + 1):
        filt_sum = filt_sum + fir_taps[k] * padded[taps_back - k:taps_back - k + num_steps]
    filtered = filt_sum.astype(jnp.bfloat16)
    filt_pad = jnp.pad(filtered.astype(jnp.float32), ((0, 0), (2, 2), (2, 2)))
    white_sum = jnp.zeros(raw_signal.shape, jnp.float32)
    for row_off in range(5):
        for col_off in range(5):
            white_sum = white_sum + white_coef[5 * row_off + col_off] * filt_pad[:, row_off:row_off + grid_rows, col_off:col_off + col_count]
    whitened = white_sum.astype(jnp.bfloat16)
    lag_len = templates.shape[1] - 1
    block_len = 8
    white_pad = jnp.pad(whitened.astype(jnp.float32), ((0, lag_len), (2, 2), (2, 2)))
    band_matrix = template_bands(templates.astype(jnp.float32), block_len)

    def score_block(i):
        window = lax.dynamic_slice_in_dim(white_pad, i * block_len, block_len + lag_len, 0)
        pieces = [window[:, row_off:row_off + grid_rows, col_off:col_off + col_count] for row_off in range(5) for col_off in range(5)]
        stacked = jnp.stack(pieces).reshape(25 * (block_len + lag_len), grid_rows * col_count)
        scores = jnp.dot(band_matrix, stacked, precision=lax.Precision.HIGHEST, preferred_element_type=jnp.float32)
        return jnp.max(scores.reshape(templates.shape[0], block_len, grid_rows * col_count), axis=0)

    best_rows = lax.map(score_block, jnp.arange(num_steps // block_len, dtype=jnp.int32))
    return whitened, best_rows.reshape(num_steps, grid_rows, col_count)
```

```python
import jax
import jax.numpy as jnp
from jax import lax
from jax.experimental import pallas as pl
from jax.experimental.pallas import tpu as pltpu
from jax.sharding import PartitionSpec as P

BLOCK = 4


def shifted_2(array, axis, by):
    size = lax.axis_size(axis)
    pairs = [(i, i + by) for i in range(size) if 0 <= i + by < size]
    return lax.ppermute(array, axis, pairs)


def with_halo(block, axis, dim, width):
    low = shifted_2(
        lax.slice_in_dim(block, block.shape[dim] - width, None, axis=dim), axis, 1
    )
    high = shifted_2(lax.slice_in_dim(block, 0, width, axis=dim), axis, -1)
    return jnp.concatenate([low, block, high], axis=dim)


def fir_band(fir_taps, num_rows):
    taps_back = fir_taps.shape[0] - 1
    span_len = num_rows + taps_back + 1
    tap_line = jnp.concatenate([fir_taps[::-1], jnp.zeros((num_rows,), jnp.float32)])
    tiled_line = jnp.tile(tap_line, num_rows)[: num_rows * (span_len - 1)]
    return tiled_line.reshape(num_rows, span_len - 1)


def filter_time(extended, fir_taps):
    taps_back = fir_taps.shape[0] - 1
    num_rows = extended.shape[0] - taps_back
    fir_matrix = fir_band(fir_taps, num_rows)
    flattened = extended.reshape(extended.shape[0], -1)
    product = jnp.dot(
        fir_matrix, flattened, precision=lax.Precision.HIGHEST, preferred_element_type=jnp.float32
    )
    return product.reshape(num_rows, extended.shape[1], extended.shape[2]).astype(jnp.bfloat16)


def whiten(rimmed, white_coef):
    row_count = white_coef.shape[1]
    col_count = white_coef.shape[2]
    padded = jnp.pad(rimmed, ((0, 0), (0, 0), (2, 2)))
    summed = jnp.zeros((rimmed.shape[0], row_count, col_count), jnp.float32)
    for row_off in range(5):
        for col_off in range(5):
            summed = summed + white_coef[5 * row_off + col_off] * padded[
                :, row_off : row_off + row_count, col_off : col_off + col_count
            ].astype(jnp.float32)
    return summed.astype(jnp.bfloat16)


def build_band(tmpl_ref, band_ref):
    spots, count, slot = tmpl_ref.shape
    flat = jnp.concatenate(
        [tmpl_ref[s].astype(jnp.float32) for s in range(spots)]
        + [jnp.zeros((count, slot), jnp.float32)] * (spots % 2),
        axis=1,
    )
    for b in range(BLOCK):
        moved = flat if b == 0 else pltpu.roll(flat, b, 1)
        band_ref[b * count : (b + 1) * count, :] = moved.astype(jnp.bfloat16)


def build_copies(row, block, copies_ref):
    span, cols = block.shape
    lane = lax.broadcasted_iota(jnp.int32, (span, cols), 1)
    for b in range(5):
        by = 2 - b
        moved = block if by == 0 else pltpu.roll(block, by % cols, 1)
        if by > 0:
            moved = jnp.where(lane >= by, moved, 0.0)
        elif by < 0:
            moved = jnp.where(lane < cols + by, moved, 0.0)
        for phase in range(4):
            late = moved if phase == 0 else pltpu.roll(moved, span - 4 * phase, 0)
            copies_ref[b, phase, row] = late.astype(jnp.bfloat16)


def correlate_block(j, copies_ref, band_ref, best_ref, slot):
    count = band_ref.shape[0] // BLOCK
    rows = best_ref.shape[1]
    cols = best_ref.shape[2]
    depth = 25 * slot
    phase = lax.rem(j, 4)
    base = pl.multiple_of((j // 4) * 16, 16)
    band = band_ref[:, :depth]
    for r in range(0, rows, 2):
        patch = jnp.concatenate(
            [
                jnp.concatenate(
                    [copies_ref[b, phase, r + e + a, pl.ds(base, slot), :] for e in range(2)], axis=1
                )
                for a in range(5)
                for b in range(5)
            ],
            axis=0,
        )
        scores = jnp.dot(band, patch, preferred_element_type=jnp.float32)
        for b in range(BLOCK):
            top = jnp.max(scores[b * count : (b + 1) * count], axis=0, keepdims=True)
            for e in range(2):
                best_ref[BLOCK * j + b, r + e : r + e + 1, :] = top[:, e * cols : (e + 1) * cols]


def correlate_kernel(ext_ref, tmpl_ref, best_ref, copies_ref, band_ref):
    slot = tmpl_ref.shape[2]
    build_band(tmpl_ref, band_ref)

    def copies(row, carry):
        build_copies(row, ext_ref[row].astype(jnp.float32), copies_ref)
        return carry

    lax.fori_loop(0, ext_ref.shape[0], copies, 0)

    def step(j, carry):
        correlate_block(j, copies_ref, band_ref, best_ref, slot)
        return carry

    lax.fori_loop(0, best_ref.shape[0] // BLOCK, step, 0)


def correlate(extended, templates, step_count):
    span, rows, cols = extended.shape
    count, tlen, spots = templates.shape
    slot = tlen + BLOCK - 1
    padded_span = -(-span // 16) * 16
    ext = jnp.pad(jnp.transpose(extended, (1, 0, 2)), ((0, 0), (0, padded_span - span), (0, 0)))
    tmpl = jnp.pad(jnp.transpose(templates, (2, 0, 1)), ((0, 0), (0, 0), (0, slot - tlen)))
    return pl.pallas_call(
        correlate_kernel,
        out_shape=jax.ShapeDtypeStruct((step_count, rows - 4, cols), jnp.float32),
        in_specs=[pl.BlockSpec(memory_space=pltpu.VMEM)] * 2,
        out_specs=pl.BlockSpec(memory_space=pltpu.VMEM),
        scratch_shapes=[
            pltpu.VMEM((5, 4, rows, padded_span, cols), jnp.bfloat16),
            pltpu.VMEM((BLOCK * count, (spots + spots % 2) * slot), jnp.bfloat16),
        ],
        compiler_params=pltpu.CompilerParams(vmem_limit_bytes=40 * 2**20),
    )(ext, tmpl)


def shards(raw_signal, fir_taps, white_coef, templates):
    step_count = raw_signal.shape[0]
    taps_back = fir_taps.shape[0] - 1
    lag_len = templates.shape[1] - 1
    prev_part = shifted_2(raw_signal[step_count - taps_back :], "tm", 1)
    filtered = filter_time(jnp.concatenate([prev_part, raw_signal]), fir_taps)
    rimmed = with_halo(filtered, "rows", 1, 2)
    whitened = whiten(rimmed, white_coef)
    widened = with_halo(whitened, "rows", 1, 2)
    next_part = shifted_2(widened[:lag_len], "tm", -1)
    extended = jnp.concatenate([widened, next_part])
    best_score = correlate(extended, templates, step_count)
    return (whitened, best_score)


def solution(mesh):
    return jax.shard_map(
        shards,
        mesh=mesh,
        in_specs=(P("tm", "rows", None), P(), P(None, "rows", None), P()),
        out_specs=(P("tm", "rows", None), P("tm", "rows", None)),
        check_vma=False,
    )
```

```python
import functools

import jax
import jax.numpy as jnp
from jax import lax
from jax.experimental import pallas as pl
from jax.experimental.pallas import tpu as pltpu
from jax.sharding import PartitionSpec as P

BLOCK = 4
EDGE = 2


def build_band(tmpl_ref, band_ref):
    spots, count, slot = tmpl_ref.shape
    flat = jnp.concatenate(
        [tmpl_ref[s].astype(jnp.float32) for s in range(spots)]
        + [jnp.zeros((count, slot), jnp.float32)] * (spots % 2),
        axis=1,
    )
    for b in range(BLOCK):
        moved = flat if b == 0 else pltpu.roll(flat, b, 1)
        band_ref[b * count : (b + 1) * count, :] = moved.astype(jnp.bfloat16)


def build_copies(row, block, copies_ref):
    span, cols = block.shape
    lane = lax.broadcasted_iota(jnp.int32, (span, cols), 1)
    for b in range(5):
        by = 2 - b
        moved = block if by == 0 else pltpu.roll(block, by % cols, 1)
        if by > 0:
            moved = jnp.where(lane >= by, moved, 0.0)
        elif by < 0:
            moved = jnp.where(lane < cols + by, moved, 0.0)
        for phase in range(4):
            late = moved if phase == 0 else pltpu.roll(moved, span - 4 * phase, 0)
            copies_ref[b, phase, row] = late.astype(jnp.bfloat16)


def correlate_block(j, copies_ref, band_ref, best_ref, slot):
    count = band_ref.shape[0] // BLOCK
    rows = best_ref.shape[1]
    cols = best_ref.shape[2]
    depth = 25 * slot
    phase = lax.rem(j, 4)
    base = pl.multiple_of((j // 4) * 16, 16)
    band = band_ref[:, :depth]
    for r in range(0, rows, 2):
        patch = jnp.concatenate(
            [
                jnp.concatenate(
                    [copies_ref[b, phase, r + e + a, pl.ds(base, slot), :] for e in range(2)], axis=1
                )
                for a in range(5)
                for b in range(5)
            ],
            axis=0,
        )
        scores = jnp.dot(band, patch, preferred_element_type=jnp.float32)
        for b in range(BLOCK):
            top = jnp.max(scores[b * count : (b + 1) * count], axis=0, keepdims=True)
            for e in range(2):
                best_ref[BLOCK * j + b, r + e : r + e + 1, :] = top[:, e * cols : (e + 1) * cols]


def filter_rows(line_ref, ext_ref, filt_ref):
    span, rows, cols = ext_ref.shape
    steps = filt_ref.shape[1]
    line = jnp.broadcast_to(line_ref[...], (steps, span))
    toeplitz = pltpu.roll(line, 0, 1, stride=1, stride_axis=0)
    flat = jnp.concatenate([ext_ref[:, r, :] for r in range(rows)], axis=1)
    product = jnp.dot(
        toeplitz, flat, precision=lax.Precision.HIGHEST, preferred_element_type=jnp.float32
    )
    for r in range(rows):
        filt_ref[2 * EDGE + r] = product[:, r * cols : (r + 1) * cols].astype(jnp.bfloat16)


def shift_columns(block, by):
    cols = block.shape[1]
    if by == 0:
        return block
    lane = lax.broadcasted_iota(jnp.int32, block.shape, 1)
    moved = pltpu.roll(block, by % cols, 1)
    keep = lane >= by if by > 0 else lane < cols + by
    return jnp.where(keep, moved, 0.0)


def whiten_rows(filt_ref, moved_ref, coef_ref, white_ref, turned_ref):
    def move(row, carry):
        block = filt_ref[row].astype(jnp.float32)
        for b in range(5):
            moved_ref[b, row] = shift_columns(block, 2 - b)
        return carry

    lax.fori_loop(0, filt_ref.shape[0], move, 0)

    def one(row):
        total = None
        for a in range(5):
            for b in range(5):
                spot = 5 * a + b
                term = coef_ref[row, spot : spot + 1, :] * moved_ref[b, row + a]
                total = term if total is None else total + term
        white_ref[0, row] = total.astype(jnp.bfloat16)
        return total

    for row in range(coef_ref.shape[0]):
        total = one(row)
        if EDGE <= row < coef_ref.shape[0] - EDGE:
            turned_ref[:, row - EDGE, :] = total


def fused_kernel(
    row_parts, time_parts, taps_back,
    raw_ref, line_ref, coef_in_ref, tmpl_ref, white_out_ref, best_ref,
    ext_ref, coef_ref, filt_ref, moved_ref, white_ref, turned_ref, copies_ref, band_ref,
    send_sem, recv_sem,
):
    steps, rows, cols = raw_ref.shape
    slot = tmpl_ref.shape[2]
    spots = coef_in_ref.shape[0]
    row_at = lax.axis_index("rows")
    time_at = lax.axis_index("tm")
    has_low = row_at > 0
    has_high = row_at < row_parts - 1
    has_prev = time_at > 0
    has_next = time_at < time_parts - 1
    low = {"rows": row_at - 1}
    high = {"rows": row_at + 1}
    prev = {"tm": time_at - 1}
    later = {"tm": time_at + 1}

    ext_ref[0:steps] = jnp.zeros((steps, rows, cols), jnp.float32)
    coef_ref[...] = jnp.zeros(coef_ref.shape, jnp.float32)
    filt_ref[0 : 2 * EDGE] = jnp.zeros((2 * EDGE, steps, cols), jnp.bfloat16)
    filt_ref[2 * EDGE + rows :] = jnp.zeros((2 * EDGE, steps, cols), jnp.bfloat16)
    white_ref[1] = jnp.zeros(white_ref.shape[1:], jnp.bfloat16)
    for r in range(rows):
        coef_ref[EDGE + r, 0:spots, :] = coef_in_ref[:, r, :]

    barrier = pltpu.get_barrier_semaphore()
    sides = ((has_low, low), (has_high, high), (has_prev, prev), (has_next, later))
    for there, where in sides:
        @pl.when(there)
        def _():
            pl.semaphore_signal(
                barrier, inc=1, device_id=where, device_id_type=pl.DeviceIdType.MESH
            )
    peers = sum(
        (at + parts - 1) // parts + (2 * parts - 2 - at) // parts
        for at, parts in ((row_at, row_parts), (time_at, time_parts))
    )
    pl.semaphore_wait(barrier, peers)

    def remote(index, source, target, where):
        return pltpu.make_async_remote_copy(
            src_ref=source,
            dst_ref=target,
            send_sem=send_sem.at[index],
            recv_sem=recv_sem.at[index],
            device_id=where,
            device_id_type=pl.DeviceIdType.MESH,
        )

    lead = steps - taps_back
    top = 2 * EDGE + rows
    raw_copy = remote(0, raw_ref.at[lead:steps], ext_ref.at[lead:steps], later)
    coef_down = remote(1, coef_ref.at[EDGE : 2 * EDGE], coef_ref.at[EDGE + rows : 2 * EDGE + rows], low)
    coef_up = remote(2, coef_ref.at[rows : EDGE + rows], coef_ref.at[0:EDGE], high)
    filt_down = remote(3, filt_ref.at[2 * EDGE : 4 * EDGE], filt_ref.at[top : top + 2 * EDGE], low)
    filt_up = remote(4, filt_ref.at[rows:top], filt_ref.at[0 : 2 * EDGE], high)
    white_copy = remote(5, white_ref.at[0], white_ref.at[1], prev)

    def start(copy, there):
        @pl.when(there)
        def _():
            copy.start()

    def sent(copy, there):
        @pl.when(there)
        def _():
            copy.wait_send()

    def arrived(copy, there):
        @pl.when(there)
        def _():
            copy.wait_recv()

    start(raw_copy, has_next)
    start(coef_down, has_low)
    start(coef_up, has_high)
    ext_ref[steps:] = raw_ref[...]
    build_band(tmpl_ref, band_ref)
    arrived(raw_copy, has_prev)
    filter_rows(line_ref, ext_ref, filt_ref)
    start(filt_down, has_low)
    start(filt_up, has_high)
    arrived(coef_down, has_high)
    arrived(coef_up, has_low)
    arrived(filt_down, has_high)
    arrived(filt_up, has_low)
    whiten_rows(filt_ref, moved_ref, coef_ref, white_ref, turned_ref)
    start(white_copy, has_prev)
    white_out_ref[...] = turned_ref[...].astype(jnp.bfloat16)
    arrived(white_copy, has_next)

    def copies(row, carry):
        block = jnp.concatenate([white_ref[0, row], white_ref[1, row]], axis=0)
        build_copies(row, block.astype(jnp.float32), copies_ref)
        return carry

    lax.fori_loop(0, rows + 2 * EDGE, copies, 0)

    def step(j, carry):
        correlate_block(j, copies_ref, band_ref, best_ref, slot)
        return carry

    lax.fori_loop(0, steps // BLOCK, step, 0)
    sent(raw_copy, has_next)
    sent(coef_down, has_low)
    sent(coef_up, has_high)
    sent(filt_down, has_low)
    sent(filt_up, has_high)
    sent(white_copy, has_prev)


def shards(raw_signal, fir_taps, white_coef, templates):
    steps, rows, cols = raw_signal.shape
    count, tlen, spots = templates.shape
    taps_back = fir_taps.shape[0] - 1
    lead = steps - taps_back
    slot = tlen + BLOCK - 1
    tmpl = jnp.pad(jnp.transpose(templates, (2, 0, 1)), ((0, 0), (0, 0), (0, slot - tlen)))
    line = jnp.pad(fir_taps[::-1], (lead, 2 * steps - lead - taps_back - 1)).reshape(1, 2 * steps)
    wide = rows + 2 * EDGE
    vmem = pl.BlockSpec(memory_space=pltpu.VMEM)
    kernel = functools.partial(
        fused_kernel, lax.axis_size("rows"), lax.axis_size("tm"), taps_back
    )
    return pl.pallas_call(
        kernel,
        out_shape=(
            jax.ShapeDtypeStruct((steps, rows, cols), jnp.bfloat16),
            jax.ShapeDtypeStruct((steps, rows, cols), jnp.float32),
        ),
        in_specs=[vmem] * 4,
        out_specs=(vmem, vmem),
        scratch_shapes=[
            pltpu.VMEM((2 * steps, rows, cols), jnp.float32),
            pltpu.VMEM((wide, 32, cols), jnp.float32),
            pltpu.VMEM((rows + 4 * EDGE, steps, cols), jnp.bfloat16),
            pltpu.VMEM((5, rows + 4 * EDGE, steps, cols), jnp.float32),
            pltpu.VMEM((2, wide, steps, cols), jnp.bfloat16),
            pltpu.VMEM((steps, rows, cols), jnp.float32),
            pltpu.VMEM((5, 4, wide, 2 * steps, cols), jnp.bfloat16),
            pltpu.VMEM((BLOCK * count, (spots + spots % 2) * slot), jnp.bfloat16),
            pltpu.SemaphoreType.DMA((6,)),
            pltpu.SemaphoreType.DMA((6,)),
        ],
        compiler_params=pltpu.CompilerParams(
            collective_id=0, has_side_effects=True, vmem_limit_bytes=48 * 2**20
        ),
    )(raw_signal, line, white_coef, tmpl)


def solution(mesh):
    return jax.shard_map(
        shards,
        mesh=mesh,
        in_specs=(P("tm", "rows", None), P(), P(None, "rows", None), P()),
        out_specs=(P("tm", "rows", None), P("tm", "rows", None)),
        check_vma=False,
    )
```

```python
import functools

import jax
import jax.numpy as jnp
from jax import lax
from jax.experimental import pallas as pl
from jax.experimental.pallas import tpu as pltpu
from jax.sharding import PartitionSpec as P

BLOCK = 4
EDGE = 2
CHUNK = 16
PAIRS = 2


def build_band(tmpl_ref, early_ref, late_ref):
    spots, count, slot = tmpl_ref.shape
    flat = jnp.concatenate(
        [tmpl_ref[s].astype(jnp.float32) for s in range(spots)]
        + [jnp.zeros((count, slot), jnp.float32)] * (spots % 2),
        axis=1,
    )
    stacked = jnp.concatenate(
        [flat] + [pltpu.roll(flat, b, 1) for b in range(1, BLOCK)], axis=0
    )
    tall = jnp.transpose(stacked)
    chunks = [
        [tall[s * slot + m * CHUNK : s * slot + (m + 1) * CHUNK] for s in range(spots)]
        for m in range(slot // CHUNK)
    ]
    blank = [tall[spots * slot :]] if spots % 2 else []
    for order, band_ref in ((chunks, early_ref), (chunks[::-1], late_ref)):
        pieces = [piece for chunk in order for piece in chunk] + blank
        band_ref[...] = jnp.transpose(jnp.concatenate(pieces, axis=0)).astype(jnp.bfloat16)


def build_copies(row, block, copies_ref, start, length):
    span = block.shape[0]
    for b in range(5):
        moved = shift_columns(block, 2 - b)
        for phase in range(CHUNK // BLOCK):
            late = moved if phase == 0 else pltpu.roll(moved, span - BLOCK * phase, 0)
            copies_ref[b, phase, row, start : start + length] = late[:length].astype(jnp.bfloat16)


def patch_of(copies_ref, phase, r, group, chunks):
    return jnp.concatenate(
        [
            jnp.concatenate(
                [
                    copies_ref[b, phase, r + e + a, (group + m) * CHUNK : (group + m + 1) * CHUNK, :]
                    for e in range(2)
                ],
                axis=1,
            )
            for m in chunks
            for a in range(5)
            for b in range(5)
        ],
        axis=0,
    )


def store_best(scores, t, r, best_ref):
    count = scores.shape[0] // BLOCK
    cols = best_ref.shape[2]
    for b in range(BLOCK):
        top = jnp.max(scores[b * count : (b + 1) * count], axis=0, keepdims=True)
        for e in range(2):
            best_ref[t + b, pl.ds(r + e, 1), :] = top[:, e * cols : (e + 1) * cols]


def correlate(phase, r, is_first, late, copies_ref, early_ref, late_ref, part_ref, best_ref, groups, total):
    pair = r // 2
    for group in range(groups):
        here = max(0, min(total, groups - group - (0 if is_first else 1)))
        t = group * CHUNK + phase * BLOCK
        depth = 25 * CHUNK
        if not late:
            if here:
                patch = patch_of(copies_ref, phase, r, group, range(here))
                scores = jnp.dot(
                    early_ref[:, : here * depth], patch, preferred_element_type=jnp.float32
                )
                if here == total:
                    store_best(scores, t, r, best_ref)
                else:
                    part_ref[group, phase, pair] = scores
        elif here < total:
            patch = patch_of(copies_ref, phase, r, group, range(total - 1, here - 1, -1))
            scores = jnp.dot(
                late_ref[:, : (total - here) * depth], patch, preferred_element_type=jnp.float32
            )
            if here:
                scores = scores + part_ref[group, phase, pair]
            store_best(scores, t, r, best_ref)


def filter_rows(line_ref, ext_ref, filt_ref):
    span, rows, cols = ext_ref.shape
    steps = filt_ref.shape[1]
    line = jnp.broadcast_to(line_ref[...], (steps, span))
    toeplitz = pltpu.roll(line, 0, 1, stride=1, stride_axis=0)
    flat = jnp.concatenate([ext_ref[:, r, :] for r in range(rows)], axis=1)
    product = jnp.dot(
        toeplitz, flat, precision=lax.Precision.HIGHEST, preferred_element_type=jnp.float32
    )
    for r in range(rows):
        filt_ref[2 * EDGE + r] = product[:, r * cols : (r + 1) * cols].astype(jnp.bfloat16)


def shift_columns(block, by):
    cols = block.shape[1]
    if by == 0:
        return block
    lane = lax.broadcasted_iota(jnp.int32, block.shape, 1)
    moved = pltpu.roll(block, by % cols, 1)
    keep = lane >= by if by > 0 else lane < cols + by
    return jnp.where(keep, moved, 0.0)


def whiten_rows(filt_ref, moved_ref, coef_ref, white_ref, turned_ref):
    def move(row, carry):
        block = filt_ref[row].astype(jnp.float32)
        for b in range(5):
            moved_ref[b, row] = shift_columns(block, 2 - b)
        return carry

    lax.fori_loop(0, filt_ref.shape[0], move, 0)

    def one(row):
        total = None
        for a in range(5):
            for b in range(5):
                spot = 5 * a + b
                term = coef_ref[row, spot : spot + 1, :] * moved_ref[b, row + a]
                total = term if total is None else total + term
        white_ref[0, row] = total.astype(jnp.bfloat16)
        return total

    for row in range(coef_ref.shape[0]):
        total = one(row)
        if EDGE <= row < coef_ref.shape[0] - EDGE:
            turned_ref[:, row - EDGE, :] = total


def fused_kernel(
    row_parts, time_parts, taps_back,
    raw_ref, line_ref, coef_in_ref, tmpl_ref, white_out_ref, best_ref,
    ext_ref, coef_ref, filt_ref, moved_ref, white_ref, turned_ref, copies_ref, early_ref, late_ref,
    part_ref,    send_sem, recv_sem,
):
    steps, rows, cols = raw_ref.shape
    slot = tmpl_ref.shape[2]
    spots = coef_in_ref.shape[0]
    row_at = lax.axis_index("rows")
    time_at = lax.axis_index("tm")
    has_low = row_at > 0
    has_high = row_at < row_parts - 1
    has_prev = time_at > 0
    has_next = time_at < time_parts - 1
    low = {"rows": row_at - 1}
    high = {"rows": row_at + 1}
    prev = {"tm": time_at - 1}
    later = {"tm": time_at + 1}

    ext_ref[0:steps] = jnp.zeros((steps, rows, cols), jnp.float32)
    coef_ref[...] = jnp.zeros(coef_ref.shape, jnp.float32)
    filt_ref[0 : 2 * EDGE] = jnp.zeros((2 * EDGE, steps, cols), jnp.bfloat16)
    filt_ref[2 * EDGE + rows :] = jnp.zeros((2 * EDGE, steps, cols), jnp.bfloat16)
    white_ref[1] = jnp.zeros(white_ref.shape[1:], jnp.bfloat16)
    for r in range(rows):
        coef_ref[EDGE + r, 0:spots, :] = coef_in_ref[:, r, :]

    barrier = pltpu.get_barrier_semaphore()
    sides = ((has_low, low), (has_high, high), (has_prev, prev), (has_next, later))
    for there, where in sides:
        @pl.when(there)
        def _():
            pl.semaphore_signal(
                barrier, inc=1, device_id=where, device_id_type=pl.DeviceIdType.MESH
            )
    peers = sum(
        (at + parts - 1) // parts + (2 * parts - 2 - at) // parts
        for at, parts in ((row_at, row_parts), (time_at, time_parts))
    )
    pl.semaphore_wait(barrier, peers)

    def remote(index, source, target, where):
        return pltpu.make_async_remote_copy(
            src_ref=source,
            dst_ref=target,
            send_sem=send_sem.at[index],
            recv_sem=recv_sem.at[index],
            device_id=where,
            device_id_type=pl.DeviceIdType.MESH,
        )

    lead = steps - taps_back
    top = 2 * EDGE + rows
    raw_copy = remote(0, raw_ref.at[lead:steps], ext_ref.at[lead:steps], later)
    coef_down = remote(1, coef_ref.at[EDGE : 2 * EDGE], coef_ref.at[EDGE + rows : 2 * EDGE + rows], low)
    coef_up = remote(2, coef_ref.at[rows : EDGE + rows], coef_ref.at[0:EDGE], high)
    filt_down = remote(3, filt_ref.at[2 * EDGE : 4 * EDGE], filt_ref.at[top : top + 2 * EDGE], low)
    filt_up = remote(4, filt_ref.at[rows:top], filt_ref.at[0 : 2 * EDGE], high)
    white_copy = remote(5, white_ref.at[0], white_ref.at[1], prev)

    def start(copy, there):
        @pl.when(there)
        def _():
            copy.start()

    def sent(copy, there):
        @pl.when(there)
        def _():
            copy.wait_send()

    def arrived(copy, there):
        @pl.when(there)
        def _():
            copy.wait_recv()

    start(raw_copy, has_next)
    start(coef_down, has_low)
    start(coef_up, has_high)
    ext_ref[steps:] = raw_ref[...]
    arrived(raw_copy, has_prev)
    filter_rows(line_ref, ext_ref, filt_ref)
    start(filt_down, has_low)
    start(filt_up, has_high)
    build_band(tmpl_ref, early_ref, late_ref)
    arrived(coef_down, has_high)
    arrived(coef_up, has_low)
    arrived(filt_down, has_high)
    arrived(filt_up, has_low)
    whiten_rows(filt_ref, moved_ref, coef_ref, white_ref, turned_ref)
    start(white_copy, has_prev)
    white_out_ref[...] = turned_ref[...].astype(jnp.bfloat16)

    def copies_here(row, carry):
        build_copies(row, white_ref[0, row].astype(jnp.float32), copies_ref, 0, steps)
        return carry

    def copies_late(row, carry):
        block = jnp.concatenate([white_ref[0, row, steps - CHUNK :], white_ref[1, row]], axis=0)
        build_copies(row, block.astype(jnp.float32), copies_ref, steps - CHUNK, slot)
        return carry

    phases = CHUNK // BLOCK
    splits = rows // (2 * PAIRS)

    def run(late):
        def work(phase, part, is_first):
            for pair in range(PAIRS):
                correlate(
                    phase, part * (2 * PAIRS) + 2 * pair, is_first, late, copies_ref,
                    early_ref, late_ref, part_ref, best_ref, steps // CHUNK, slot // CHUNK,
                )

        def first(part, carry):
            work(0, part, True)
            return carry

        def others(i, carry):
            work(1 + i // splits, i % splits, False)
            return carry

        lax.fori_loop(0, splits, first, 0)
        lax.fori_loop(0, (phases - 1) * splits, others, 0)

    lax.fori_loop(0, rows + 2 * EDGE, copies_here, 0)
    run(False)
    arrived(white_copy, has_next)
    lax.fori_loop(0, rows + 2 * EDGE, copies_late, 0)
    run(True)
    sent(raw_copy, has_next)
    sent(coef_down, has_low)
    sent(coef_up, has_high)
    sent(filt_down, has_low)
    sent(filt_up, has_high)
    sent(white_copy, has_prev)


def shards(raw_signal, fir_taps, white_coef, templates):
    steps, rows, cols = raw_signal.shape
    count, tlen, spots = templates.shape
    taps_back = fir_taps.shape[0] - 1
    lead = steps - taps_back
    slot = tlen + BLOCK - 1
    tmpl = jnp.pad(jnp.transpose(templates, (2, 0, 1)), ((0, 0), (0, 0), (0, slot - tlen)))
    line = jnp.pad(fir_taps[::-1], (lead, 2 * steps - lead - taps_back - 1)).reshape(1, 2 * steps)
    wide = rows + 2 * EDGE
    vmem = pl.BlockSpec(memory_space=pltpu.VMEM)
    kernel = functools.partial(
        fused_kernel, lax.axis_size("rows"), lax.axis_size("tm"), taps_back
    )
    return pl.pallas_call(
        kernel,
        out_shape=(
            jax.ShapeDtypeStruct((steps, rows, cols), jnp.bfloat16),
            jax.ShapeDtypeStruct((steps, rows, cols), jnp.float32),
        ),
        in_specs=[vmem] * 4,
        out_specs=(vmem, vmem),
        scratch_shapes=[
            pltpu.VMEM((2 * steps, rows, cols), jnp.float32),
            pltpu.VMEM((wide, 32, cols), jnp.float32),
            pltpu.VMEM((rows + 4 * EDGE, steps, cols), jnp.bfloat16),
            pltpu.VMEM((5, rows + 4 * EDGE, steps, cols), jnp.float32),
            pltpu.VMEM((2, wide, steps, cols), jnp.bfloat16),
            pltpu.VMEM((steps, rows, cols), jnp.float32),
            pltpu.VMEM((5, CHUNK // BLOCK, wide, steps + slot - CHUNK, cols), jnp.bfloat16),
            pltpu.VMEM((BLOCK * count, (spots + spots % 2) * slot), jnp.bfloat16),
            pltpu.VMEM((BLOCK * count, (spots + spots % 2) * slot), jnp.bfloat16),
            pltpu.VMEM(
                (steps // CHUNK, CHUNK // BLOCK, rows // 2, BLOCK * count, 2 * cols), jnp.float32
            ),
            pltpu.SemaphoreType.DMA((6,)),
            pltpu.SemaphoreType.DMA((6,)),
        ],
        compiler_params=pltpu.CompilerParams(
            collective_id=0, has_side_effects=True, vmem_limit_bytes=48 * 2**20
        ),
    )(raw_signal, line, white_coef, tmpl)


def solution(mesh):
    return jax.shard_map(
        shards,
        mesh=mesh,
        in_specs=(P("tm", "rows", None), P(), P(None, "rows", None), P()),
        out_specs=(P("tm", "rows", None), P("tm", "rows", None)),
        check_vma=False,
    )
```
